1024 devices in a mesh: dp: 64 (over z_lo, x, core), seq: 16 (over z_hi, y).
Axes of the slice: x: 4, y: 4, z: 32 (z_hi: 4, z_lo: 8; z = z_hi * 8 + z_lo), core: 2. Of those that a mesh axis runs over, the one named last changes fastest.
Arguments:
- queries: bfloat16 [131072, 4096], P(('dp', 'seq')), may hold values from -300 to 300
- key_proj: bfloat16 [131072, 512], P(('dp', 'seq')), may hold values from -4.5 to 4.5
- value_proj: bfloat16 [131072, 512], P(('dp', 'seq')), may hold values from -6 to 6
- seq_lengths: int32 [256], replicated, may hold values from 1 to 1025, 131072 in all
Outputs:
- attended: bfloat16 [131072, 4096], P(('dp', 'seq'))
The draws below stay inside these ranges and needn't reach their ends.
Inputs may be any that keep to these rules, and one draw needn't show every extreme that they name: `seq_lengths`: the sequences cover all 131072 tokens; the longest has exactly 1025 tokens.
All inputs are finite; a program needn't handle non-finite values.
Results may differ from the reference program's by a relative error of at most 0.0036.
Values may be sent and summed in bfloat16 or wider, within the bound.
A program may use at most 32 MiB of HBM per device.

```python
import math
import jax
import jax.numpy as jnp
import numpy as np
from jax import lax

HD = 128
QH = 32
KVH = 4
BLOCK = 2048
REACH = 1024
TOKENS = 131072
COUNT = 256


def normal_keys(key):
    return jax.random.truncated_normal(jax.random.fold_in(key, 11), -4.5, 4.5, (TOKENS, KVH * HD), jnp.float32)


def draw_key_proj(key, part):
    return normal_keys(key).astype(jnp.bfloat16)


def draw_queries(key, part):
    drawn = jax.random.truncated_normal(jax.random.fold_in(key, 12), -4.5, 4.5, (TOKENS, QH * HD), jnp.float32)
    return drawn.astype(jnp.bfloat16)


def block_scale(own_key, dims, split, smallest, top_value):
    def one(axis_at, shards_of):
        heights = jax.random.uniform(jax.random.fold_in(jax.random.fold_in(own_key, 6), axis_at), (shards_of,), jnp.float32, smallest / len(split), top_value / len(split))
        return jnp.repeat(jnp.exp(heights), dims[axis_at] // shards_of).reshape((-1,) + (1,) * (len(dims) - axis_at - 1))

    loudness = one(*split[0])
    for cut in split[1:]:
        loudness = loudness * one(*cut)
    return loudness


def profile(count, total, most, slope):
    portions = [(1 << 20) // math.isqrt(standing ** slope) + 1 for standing in range(2, count + 1)]
    rest, counts = total - most - (count - 1), [1] * (count - 1)
    while rest > 0:
        free = [i for i in range(count - 1) if counts[i] < most]
        mass, left = sum([portions[i] for i in free]), rest
        for i in free:
            extra = min(most - counts[i], max(1, left * portions[i] // mass), rest)
            counts[i] = counts[i] + extra
            rest = rest - extra
    return np.array([most] + counts)


def ragged_sizes(key, count, total, most, slope):
    if count == 2:
        one = jax.random.randint(key, (), max(1, total - most), min(most, total - 1) + 1)
        return jnp.stack([one, total - one])
    lengths = jnp.asarray(profile(count, total, most, slope), jnp.int32)
    twos = (count - 1) // 2
    giver, receiver = lengths[1:1 + 2 * twos:2], lengths[2:2 + 2 * twos:2]
    slack = jnp.minimum(giver - 1, most - receiver)
    passed = jax.random.randint(jax.random.fold_in(key, 1), (twos,), 0, 1 << 20) % (slack + 1)
    lengths = lengths.at[1:1 + 2 * twos:2].set(giver - passed).at[2:2 + 2 * twos:2].set(receiver + passed)
    return lengths[jax.random.permutation(jax.random.fold_in(key, 2), count)]


def gaussian(key, extent, scale, limit, split=(), held_as=jnp.bfloat16):
    result = jax.random.normal(key, extent, jnp.float32) * scale
    if len(split) > 0:
        result = block_scale(key, extent, split, -0.22, 0.18) * result
    return jnp.clip(result, min=-limit, max=limit).astype(held_as)


def setup_inputs(seed: int = 0) -> dict:
    keys = jax.random.split(jax.random.key(seed), 5)
    queries = draw_queries(jax.random.fold_in(keys[4], 71), 0)
    key_proj = draw_key_proj(jax.random.fold_in(keys[4], 71), 0)
    value_proj = gaussian(keys[2], (TOKENS, KVH * HD), 1.0, 6.0, ((0, 1024),))
    seq_lengths = ragged_sizes(keys[3], COUNT, TOKENS, REACH + 1, 1).astype(jnp.int32)
    return {"queries": queries, "key_proj": key_proj, "value_proj": value_proj, "seq_lengths": seq_lengths}


score_scale = 0.08838834764831845
neg_fill = -1e30


def reference(queries, key_proj, value_proj, seq_lengths):
    tile_rows = math.gcd(BLOCK, 512)
    group_size = QH // KVH
    query_all = queries.reshape(TOKENS, QH, HD)
    keys_padded = jnp.concatenate([jnp.zeros((REACH, KVH, HD), jnp.bfloat16), key_proj.reshape(TOKENS, KVH, HD)], axis=0)
    values_padded = jnp.concatenate([jnp.zeros((REACH, KVH, HD), jnp.bfloat16), value_proj.reshape(TOKENS, KVH, HD)], axis=0)
    seq_ends = jnp.cumsum(seq_lengths).astype(jnp.int32)
    begins = (seq_ends - seq_lengths).astype(jnp.int32)
    window = tile_rows + REACH

    def one_tile(tile_index):
        offset = (tile_index * tile_rows).astype(jnp.int32)
        query_tile = lax.dynamic_slice_in_dim(query_all, offset, tile_rows, 0).astype(jnp.float32)
        key_window = lax.dynamic_slice_in_dim(keys_padded, offset, window, 0)
        value_window = lax.dynamic_slice_in_dim(values_padded, offset, window, 0)
        query_pos = offset + jnp.arange(tile_rows, dtype=jnp.int32)
        key_pos = offset - REACH + jnp.arange(window, dtype=jnp.int32)
        covered = begins[None, :] <= query_pos[:, None]
        starts = jnp.max(jnp.where(covered, begins[None, :], 0), axis=1).astype(jnp.int32)
        allowed = (key_pos[None, :] <= query_pos[:, None]) & (key_pos[None, :] >= starts[:, None])
        key_heads = jnp.repeat(key_window, group_size, axis=1).astype(jnp.float32)
        value_heads = jnp.repeat(value_window, group_size, axis=1).astype(jnp.float32)
        scores = jnp.einsum('qhd,khd->hqk', query_tile, key_heads) * score_scale
        scores = jnp.where(allowed[None], scores, neg_fill)
        row_max = jnp.max(scores, axis=2, keepdims=True)
        weights = jnp.where(allowed[None], jnp.exp(scores - row_max), 0.0)
        row_sum = jnp.sum(weights, axis=2)
        rounded = lax.optimization_barrier(weights.astype(jnp.bfloat16)).astype(jnp.float32)
        mixed = jnp.einsum('hqk,khd->hqd', rounded, value_heads) / row_sum[..., None]
        return jnp.transpose(mixed, (1, 0, 2)).reshape(tile_rows, QH * HD).astype(jnp.bfloat16)

    pieces = lax.map(one_tile, jnp.arange(TOKENS // tile_rows, dtype=jnp.int32))
    return pieces.reshape(TOKENS, QH * HD)
```

```python
import functools

import jax
import jax.numpy as jnp
from jax import lax
from jax.experimental import pallas as pl
from jax.experimental.pallas import tpu as pltpu
from jax.sharding import PartitionSpec as P

HD = 128
QH = 32
KVH = 4
GROUP = QH // KVH
ROWS = 128
SLOTS = 9
AHEAD = 80
SCALE = 0.08838834764831845 * 1.4426950408889634
MASKED = -1e30
MESH = pl.DeviceIdType.MESH


def kernel(
    seq_size,
    total,
    len_ref,
    q_ref,
    k_ref,
    v_ref,
    o_ref,
    q_own,
    window,
    transit,
    scores,
    weights,
    peaks,
    inverse,
    bias,
    local_sem,
    z_send,
    y_send,
    arrived,
    passing,
):
    dp = lax.axis_index("dp")
    seq = lax.axis_index("seq")
    chunk = dp * seq_size + seq
    lane_y = seq % 4

    def at_chunk(offset):
        other = (chunk + offset + total) % total
        return (other // seq_size, other % seq_size)

    def at_y(turn):
        return (dp, seq - lane_y + (lane_y + turn) % 4)

    own = [
        pltpu.make_async_copy(q_ref, q_own, local_sem.at[0]),
        pltpu.make_async_copy(k_ref, window.at[0, 0], local_sem.at[1]),
        pltpu.make_async_copy(v_ref, window.at[1, 0], local_sem.at[2]),
    ]
    for copy in own:
        copy.start()

    barrier = pltpu.get_barrier_semaphore()
    for device in (at_chunk(-4), at_chunk(4), at_chunk(-12), at_y(1), at_y(2), at_y(3)):
        pl.semaphore_signal(barrier, inc=1, device_id=device, device_id_type=MESH)
    pl.semaphore_wait(barrier, 6)

    parts = (pl.ds(0, AHEAD), pl.ds(AHEAD, ROWS - AHEAD))
    mine = (k_ref, v_ref)

    def z_copy(kv, step):
        src, dst, recv, device = (
            (mine[kv].at[parts[0]], window.at[kv, 4, parts[0]], arrived.at[kv, 4, 0], at_chunk(4)),
            (mine[kv].at[parts[1]], transit.at[kv], passing.at[kv], at_chunk(-4)),
            (window.at[kv, 4, parts[0]], window.at[kv, 8, parts[0]], arrived.at[kv, 8, 0], at_chunk(4)),
            (transit.at[kv], window.at[kv, 8, parts[1]], arrived.at[kv, 8, 1], at_chunk(12)),
            (window.at[kv, 8, parts[1]], window.at[kv, 4, parts[1]], arrived.at[kv, 4, 1], at_chunk(-4)),
        )[step]
        return pltpu.make_async_remote_copy(
            src_ref=src,
            dst_ref=dst,
            send_sem=z_send.at[kv, step],
            recv_sem=recv,
            device_id=device,
            device_id_type=MESH,
        )

    def y_copy(kv, part, turn, message, src):
        slot = turn + 4 * message
        return pltpu.make_async_remote_copy(
            src_ref=src,
            dst_ref=window.at[kv, slot, parts[part]],
            send_sem=y_send.at[kv, turn - 1, message, part],
            recv_sem=arrived.at[kv, slot, part],
            device_id=at_y(turn),
            device_id_type=MESH,
        )

    def share(kv, part, slot):
        for turn in (1, 2, 3):
            ahead = lane_y + turn < 4
            src = mine[kv].at[parts[part]] if slot == 0 else window.at[kv, slot, parts[part]]
            if slot == 0 or slot == 4:
                @pl.when(ahead)
                def _():
                    y_copy(kv, part, turn, slot // 4, src).start()
            if slot == 4 or slot == 8:
                @pl.when(jnp.logical_not(ahead))
                def _():
                    y_copy(kv, part, turn, slot // 4 - 1, src).start()

    def wait_arrival(kv, slot, part):
        ref = window.at[kv, slot, parts[part]]
        pltpu.make_async_copy(ref, ref, arrived.at[kv, slot, part]).wait()

    def wait_passing(kv):
        pltpu.make_async_copy(transit.at[kv], transit.at[kv], passing.at[kv]).wait()

    for kv in (0, 1):
        z_copy(kv, 0).start()
        z_copy(kv, 1).start()
    for kv in (0, 1):
        for part in (0, 1):
            share(kv, part, 0)

    lengths = len_ref[...]
    count = lengths.shape[1]
    down = lax.broadcasted_iota(jnp.int32, (count, count), 0)
    across = lax.broadcasted_iota(jnp.int32, (count, count), 1)
    column = jnp.sum(jnp.where(down == across, lengths, 0), axis=1, keepdims=True)
    begins = jnp.sum(jnp.where(down < across, column, 0), axis=0, keepdims=True)
    base = chunk * ROWS
    positions = base + lax.broadcasted_iota(jnp.int32, (ROWS, 1), 0)
    starts = jnp.max(jnp.where(begins <= positions, begins, 0), axis=1, keepdims=True)
    key_lane = base + lax.broadcasted_iota(jnp.int32, (ROWS, ROWS), 1)
    for slot in range(SLOTS):
        keys_at = key_lane - slot * ROWS
        allowed = keys_at >= starts
        if slot == 0:
            allowed = allowed & (keys_at <= positions)
        bias[slot] = jnp.where(allowed, 0.0, MASKED)

    for copy in own:
        copy.wait()

    def score(first, slots, fresh):
        @pl.loop(0, KVH)
        def _(head):
            column = pl.multiple_of(head * HD, HD)
            stacked = jnp.concatenate(
                [q_own[:, pl.ds(pl.multiple_of(head * GROUP * HD + j * HD, HD), HD)] for j in range(GROUP)],
                axis=0,
            )
            peak = None if fresh else peaks[head]
            keys = window[0, pl.ds(first, slots), :, pl.ds(column, HD)].reshape(slots * ROWS, HD)
            raw = lax.dot_general(
                stacked, keys, (((1,), (1,)), ((), ())), preferred_element_type=jnp.float32
            ).reshape(GROUP, ROWS, slots * ROWS)
            for i in range(slots):
                masked = raw[:, :, i * ROWS : (i + 1) * ROWS] + bias[first + i][None]
                scores[first + i, head] = masked
                peak = masked if peak is None else jnp.maximum(peak, masked)
            peaks[head] = peak

    score(0, 1, True)

    for kv in (0, 1):
        wait_arrival(kv, 4, 0)
        z_copy(kv, 2).start()
        share(kv, 0, 4)
        wait_passing(kv)
        z_copy(kv, 3).start()
    for kv in (0, 1):
        wait_arrival(kv, 8, 1)
        z_copy(kv, 4).start()
        share(kv, 1, 8)
    for kv in (0, 1):
        wait_arrival(kv, 8, 0)
        share(kv, 0, 8)
        wait_arrival(kv, 4, 1)
        share(kv, 1, 4)

    for slot in (1, 2, 3, 5, 6, 7):
        for part in (0, 1):
            wait_arrival(0, slot, part)
    for first in (1, 3, 5, 7):
        score(first, 2, False)

    @pl.loop(0, QH)
    def _(index):
        head, j = index // GROUP, index % GROUP
        peak = jnp.max(peaks[head, j], axis=1, keepdims=True)
        total_weight = jnp.zeros((ROWS, ROWS), jnp.float32)
        for slot in range(SLOTS):
            weight = jnp.exp2((scores[slot, head, j] - peak) * SCALE)
            total_weight = total_weight + weight
            weights[head, j, :, slot * ROWS : (slot + 1) * ROWS] = weight.astype(jnp.bfloat16)
        row_sum = jnp.sum(total_weight, axis=1, keepdims=True)
        inverse[index] = jnp.broadcast_to(1.0 / row_sum, (ROWS, HD))

    for slot in (1, 2, 3, 5, 6, 7):
        for part in (0, 1):
            wait_arrival(1, slot, part)

    @pl.loop(0, KVH)
    def _(head):
        column = pl.multiple_of(head * HD, HD)
        values = window[1, :, :, pl.ds(column, HD)].reshape(SLOTS * ROWS, HD)
        mixed = jnp.dot(
            weights[head].reshape(GROUP * ROWS, SLOTS * ROWS), values, preferred_element_type=jnp.float32
        )
        for j in range(GROUP):
            place = pl.multiple_of(head * GROUP * HD + j * HD, HD)
            o_ref[:, pl.ds(place, HD)] = (
                mixed[j * ROWS : (j + 1) * ROWS] * inverse[head * GROUP + j]
            ).astype(jnp.bfloat16)

    for kv in (0, 1):
        for step in range(5):
            z_copy(kv, step).wait_send()
        for turn in (1, 2, 3):
            for message in (0, 1):
                for part in (0, 1):
                    y_copy(kv, part, turn, message, window.at[kv, 4, parts[part]]).wait_send()


def body(queries, key_proj, value_proj, seq_lengths):
    seq_size = lax.axis_size("seq")
    total = lax.axis_size("dp") * seq_size
    rows_behind = ROWS - AHEAD
    return pl.pallas_call(
        functools.partial(kernel, seq_size, total),
        out_shape=jax.ShapeDtypeStruct((ROWS, QH * HD), jnp.bfloat16),
        in_specs=[
            pl.BlockSpec(memory_space=pltpu.VMEM),
            pl.BlockSpec(memory_space=pl.ANY),
            pl.BlockSpec(memory_space=pl.ANY),
            pl.BlockSpec(memory_space=pl.ANY),
        ],
        out_specs=pl.BlockSpec(memory_space=pltpu.VMEM),
        scratch_shapes=[
            pltpu.VMEM((ROWS, QH * HD), jnp.bfloat16),
            pltpu.VMEM((2, SLOTS, ROWS, KVH * HD), jnp.bfloat16),
            pltpu.VMEM((2, rows_behind, KVH * HD), jnp.bfloat16),
            pltpu.VMEM((SLOTS, KVH, GROUP, ROWS, ROWS), jnp.float32),
            pltpu.VMEM((KVH, GROUP, ROWS, SLOTS * ROWS), jnp.bfloat16),
            pltpu.VMEM((KVH, GROUP, ROWS, ROWS), jnp.float32),
            pltpu.VMEM((QH, ROWS, HD), jnp.float32),
            pltpu.VMEM((SLOTS, ROWS, ROWS), jnp.float32),
            pltpu.SemaphoreType.DMA((3,)),
            pltpu.SemaphoreType.DMA((2, 5)),
            pltpu.SemaphoreType.DMA((2, 3, 2, 2)),
            pltpu.SemaphoreType.DMA((2, SLOTS, 2)),
            pltpu.SemaphoreType.DMA((2,)),
        ],
        compiler_params=pltpu.CompilerParams(
            collective_id=0, has_side_effects=True, vmem_limit_bytes=52 * 2**20
        ),
    )(seq_lengths.reshape(1, -1), queries, key_proj, value_proj)


def solution(mesh):
    return jax.shard_map(
        body,
        mesh=mesh,
        in_specs=(P(("dp", "seq"), None), P(("dp", "seq"), None), P(("dp", "seq"), None), P()),
        out_specs=P(("dp", "seq"), None),
        check_vma=False,
    )
```

```python
import functools

import jax
import jax.numpy as jnp
from jax import lax
from jax.experimental import pallas as pl
from jax.experimental.pallas import tpu as pltpu
from jax.sharding import PartitionSpec as P

HD = 128
QH = 32
KVH = 4
GROUP = QH // KVH
ROWS = 128
SLOTS = 9
FORWARD = ((0, 48), (48, 32))
BACKWARD = ((80, 32), (112, 16))
BACK_FIRST = BACKWARD[0][0]
SCALE = 0.08838834764831845 * 1.4426950408889634
MASKED = -1e30
MESH = pl.DeviceIdType.MESH


AHEAD_TIMES = ((0.25, 0.55), (0.75, 1.0))
BACK_TIMES = ((0.17, 0.37, 0.57), (0.67, 0.83, 1.0))


def schedule():
    events = []
    for what, pieces, times in (("ahead", FORWARD, AHEAD_TIMES), ("back", BACKWARD, BACK_TIMES)):
        for kv in (0, 1):
            for hop, time in enumerate(times[kv]):
                for i in range(len(pieces)):
                    events.append((time - 0.12 * (1 - (i + 1) / len(pieces)), what, kv, hop, i))
    return [event[1:] for event in sorted(events)]


def kernel(
    seq_size,
    total,
    len_ref,
    q_ref,
    k_ref,
    v_ref,
    o_ref,
    q_own,
    window,
    transit,
    scores,
    weights,
    peaks,
    inverse,
    bias,
    local_sem,
    z_send,
    y_send,
    ahead_sem,
    back_sem,
    y_sem,
):
    dp = lax.axis_index("dp")
    seq = lax.axis_index("seq")
    chunk = dp * seq_size + seq
    lane_y = seq % 4

    def at_chunk(offset):
        other = (chunk + offset + total) % total
        return (other // seq_size, other % seq_size)

    def at_y(turn):
        return (dp, seq - lane_y + (lane_y + turn) % 4)

    own = [
        pltpu.make_async_copy(q_ref, q_own, local_sem.at[0]),
        pltpu.make_async_copy(k_ref, window.at[0, 0], local_sem.at[1]),
        pltpu.make_async_copy(v_ref, window.at[1, 0], local_sem.at[2]),
    ]
    for copy in own:
        copy.start()

    barrier = pltpu.get_barrier_semaphore()
    for device in (at_chunk(-4), at_chunk(4), at_chunk(-12), at_y(1), at_y(2), at_y(3)):
        pl.semaphore_signal(barrier, inc=1, device_id=device, device_id_type=MESH)

    mine = (k_ref, v_ref)

    def passing_rows(piece):
        first, count = piece
        return pl.ds(first - BACK_FIRST, count)

    def send_ahead(kv, hop, i):
        rows = pl.ds(*FORWARD[i])
        pltpu.make_async_remote_copy(
            src_ref=mine[kv].at[rows] if hop == 0 else window.at[kv, 4, rows],
            dst_ref=window.at[kv, 4 + 4 * hop, rows],
            send_sem=z_send.at[kv, hop],
            recv_sem=ahead_sem.at[kv, hop, i],
            device_id=at_chunk(4),
            device_id_type=MESH,
        ).start()

    def send_back(kv, hop, i):
        rows = pl.ds(*BACKWARD[i])
        passed = transit.at[kv, passing_rows(BACKWARD[i])]
        pltpu.make_async_remote_copy(
            src_ref=(mine[kv].at[rows], passed, window.at[kv, 8, rows])[hop],
            dst_ref=(passed, window.at[kv, 8, rows], window.at[kv, 4, rows])[hop],
            send_sem=z_send.at[kv, hop],
            recv_sem=back_sem.at[kv, hop, i],
            device_id=at_chunk((-4, 12, -4)[hop]),
            device_id_type=MESH,
        ).start()

    def y_copy(kv, turn, message, src, rows):
        slot = turn + 4 * message
        return pltpu.make_async_remote_copy(
            src_ref=src,
            dst_ref=window.at[kv, slot, rows],
            send_sem=y_send.at[kv, turn - 1, message],
            recv_sem=y_sem.at[kv, slot],
            device_id=at_y(turn),
            device_id_type=MESH,
        )

    def share(kv, slot, rows):
        src = mine[kv].at[rows] if slot == 0 else window.at[kv, slot, rows]
        for turn in (1, 2, 3):
            ahead = lane_y + turn < 4
            if slot < 8:

                @pl.when(ahead)
                def _():
                    y_copy(kv, turn, slot // 4, src, rows).start()

            if slot > 0:

                @pl.when(jnp.logical_not(ahead))
                def _():
                    y_copy(kv, turn, slot // 4 - 1, src, rows).start()

    def arrive(what, kv, hop, i):
        rows = pl.ds(*(FORWARD if what == "ahead" else BACKWARD)[i])
        if what == "ahead":
            ref = window.at[kv, 4 + 4 * hop, rows]
            pltpu.make_async_copy(ref, ref, ahead_sem.at[kv, hop, i]).wait()
            if hop == 0:
                send_ahead(kv, 1, i)
                if kv == 0:
                    send_ahead(1, 0, i)
            share(kv, 4 + 4 * hop, rows)
        else:
            ref = (
                transit.at[kv, passing_rows(BACKWARD[i])],
                window.at[kv, 8, rows],
                window.at[kv, 4, rows],
            )[hop]
            pltpu.make_async_copy(ref, ref, back_sem.at[kv, hop, i]).wait()
            if hop < 2:
                send_back(kv, hop + 1, i)
                if kv == 0 and hop == 0:
                    send_back(1, 0, i)
            if hop > 0:
                share(kv, 12 - 4 * hop, rows)

    def await_slot(kv, slot):
        ref = window.at[kv, slot]
        pltpu.make_async_copy(ref, ref, y_sem.at[kv, slot]).wait()

    lengths = len_ref[...]
    count = lengths.shape[1]
    down = lax.broadcasted_iota(jnp.int32, (count, count), 0)
    across = lax.broadcasted_iota(jnp.int32, (count, count), 1)
    column = jnp.sum(jnp.where(down == across, lengths, 0), axis=1, keepdims=True)
    begins = jnp.sum(jnp.where(down < across, column, 0), axis=0, keepdims=True)
    base = chunk * ROWS
    positions = base + lax.broadcasted_iota(jnp.int32, (ROWS, 1), 0)
    starts = jnp.max(jnp.where(begins <= positions, begins, 0), axis=1, keepdims=True)
    key_lane = base + lax.broadcasted_iota(jnp.int32, (ROWS, ROWS), 1)
    for slot in range(SLOTS):
        keys_at = key_lane - slot * ROWS
        allowed = keys_at >= starts
        if slot == 0:
            allowed = allowed & (keys_at <= positions)
        bias[slot] = jnp.where(allowed, 0.0, MASKED)

    pl.semaphore_wait(barrier, 6)
    for i in range(len(FORWARD)):
        send_ahead(0, 0, i)
    for i in range(len(BACKWARD)):
        send_back(0, 0, i)
    for kv in (0, 1):
        share(kv, 0, pl.ds(0, ROWS))

    for copy in own:
        copy.wait()

    def score(first, slots):
        @pl.loop(0, KVH)
        def _(head):
            column = pl.multiple_of(head * HD, HD)
            stacked = jnp.concatenate(
                [q_own[:, pl.ds(pl.multiple_of(head * GROUP * HD + j * HD, HD), HD)] for j in range(GROUP)],
                axis=0,
            )
            peak = None if first == 0 else peaks[head]
            keys = window[0, pl.ds(first, slots), :, pl.ds(column, HD)].reshape(slots * ROWS, HD)
            raw = lax.dot_general(
                stacked, keys, (((1,), (1,)), ((), ())), preferred_element_type=jnp.float32
            ).reshape(GROUP, ROWS, slots * ROWS)
            for i in range(slots):
                masked = raw[:, :, i * ROWS : (i + 1) * ROWS] + bias[first + i][None]
                scores[first + i, head] = masked
                peak = masked if peak is None else jnp.maximum(peak, masked)
            peaks[head] = peak

    def weigh(head):
        @pl.loop(0, GROUP)
        def _(j):
            peak = jnp.max(peaks[head, j], axis=1, keepdims=True)
            total_weight = jnp.zeros((ROWS, ROWS), jnp.float32)
            for slot in range(SLOTS):
                weight = jnp.exp2((scores[slot, head, j] - peak) * SCALE)
                total_weight = total_weight + weight
                weights[head, j, :, slot * ROWS : (slot + 1) * ROWS] = weight.astype(jnp.bfloat16)
            row_sum = jnp.sum(total_weight, axis=1, keepdims=True)
            inverse[head * GROUP + j] = jnp.broadcast_to(1.0 / row_sum, (ROWS, HD))

    score(0, 1)

    def mix(head, slots):
        values = jnp.concatenate([window[1, slot, :, pl.ds(pl.multiple_of(head * HD, HD), HD)] for slot in slots], axis=0)
        shares = jnp.concatenate([weights[head, :, :, slot * ROWS : (slot + 1) * ROWS] for slot in slots], axis=2)
        return jnp.dot(
            shares.reshape(GROUP * ROWS, len(slots) * ROWS), values, preferred_element_type=jnp.float32
        ).reshape(GROUP, ROWS, HD)

    events = schedule()
    keys_last = max(i for i, event in enumerate(events) if event[1] == 0)
    work = [functools.partial(score, first, 2) for first in (1, 3, 5, 7)]
    work += [functools.partial(weigh, head) for head in range(KVH)]
    last = [i for i in range(keys_last, len(events)) if events[i][2] < 2 - (events[i][0] == "ahead")]
    for i, event in enumerate(events):
        arrive(*event)
        if i == keys_last:
            for slot in (1, 2, 3, 5, 6, 7):
                await_slot(0, slot)
        if i in last:
            done = 8 * (last.index(i) + 1) // len(last) - 8 * last.index(i) // len(last)
            for _ in range(done):
                work.pop(0)()
    for step in work:
        step()

    along_y = (1, 2, 3, 5, 6, 7)

    @pl.loop(0, KVH)
    def _(head):
        peaks[head] = mix(head, (0, 4, 8))

    for slot in along_y:
        await_slot(1, slot)

    @pl.loop(0, KVH)
    def _(head):
        mixed = peaks[head] + mix(head, along_y)
        for j in range(GROUP):
            place = pl.multiple_of(head * GROUP * HD + j * HD, HD)
            o_ref[:, pl.ds(place, HD)] = (mixed[j] * inverse[head * GROUP + j]).astype(jnp.bfloat16)

    for kv in (0, 1):
        whole = window.at[kv, 0]
        for hop in (0, 1):
            pltpu.make_async_copy(whole, whole, z_send.at[kv, hop]).wait()
        pltpu.make_async_copy(transit.at[kv], transit.at[kv], z_send.at[kv, 2]).wait()
        for turn in (1, 2, 3):
            for message in (0, 1):
                pltpu.make_async_copy(whole, whole, y_send.at[kv, turn - 1, message]).wait()


def body(queries, key_proj, value_proj, seq_lengths):
    seq_size = lax.axis_size("seq")
    total = lax.axis_size("dp") * seq_size
    return pl.pallas_call(
        functools.partial(kernel, seq_size, total),
        out_shape=jax.ShapeDtypeStruct((ROWS, QH * HD), jnp.bfloat16),
        in_specs=[
            pl.BlockSpec(memory_space=pltpu.VMEM),
            pl.BlockSpec(memory_space=pl.ANY),
            pl.BlockSpec(memory_space=pl.ANY),
            pl.BlockSpec(memory_space=pl.ANY),
        ],
        out_specs=pl.BlockSpec(memory_space=pltpu.VMEM),
        scratch_shapes=[
            pltpu.VMEM((ROWS, QH * HD), jnp.bfloat16),
            pltpu.VMEM((2, SLOTS, ROWS, KVH * HD), jnp.bfloat16),
            pltpu.VMEM((2, ROWS - BACK_FIRST, KVH * HD), jnp.bfloat16),
            pltpu.VMEM((SLOTS, KVH, GROUP, ROWS, ROWS), jnp.float32),
            pltpu.VMEM((KVH, GROUP, ROWS, SLOTS * ROWS), jnp.bfloat16),
            pltpu.VMEM((KVH, GROUP, ROWS, ROWS), jnp.float32),
            pltpu.VMEM((QH, ROWS, HD), jnp.float32),
            pltpu.VMEM((SLOTS, ROWS, ROWS), jnp.float32),
            pltpu.SemaphoreType.DMA((3,)),
            pltpu.SemaphoreType.DMA((2, 3)),
            pltpu.SemaphoreType.DMA((2, 3, 2)),
            pltpu.SemaphoreType.DMA((2, 2, len(FORWARD))),
            pltpu.SemaphoreType.DMA((2, 3, len(BACKWARD))),
            pltpu.SemaphoreType.DMA((2, SLOTS)),
        ],
        compiler_params=pltpu.CompilerParams(
            collective_id=0, has_side_effects=True, vmem_limit_bytes=60 * 2**20
        ),
    )(seq_lengths.reshape(1, -1), queries, key_proj, value_proj)


def solution(mesh):
    return jax.shard_map(
        body,
        mesh=mesh,
        in_specs=(P(("dp", "seq"), None), P(("dp", "seq"), None), P(("dp", "seq"), None), P()),
        out_specs=P(("dp", "seq"), None),
        check_vma=False,
    )
```

```python
import functools

import jax
import jax.numpy as jnp
from jax import lax
from jax.experimental import pallas as pl
from jax.experimental.pallas import tpu as pltpu
from jax.sharding import PartitionSpec as P

HD = 128
QH = 32
KVH = 4
GROUP = QH // KVH
ROWS = 128
SLOTS = 9
FORWARD = ((0, 48), (48, 32))
BACKWARD = ((80, 32), (112, 16))
BACK_FIRST = BACKWARD[0][0]
SCALE = 0.08838834764831845 * 1.4426950408889634
MASKED = -1e30
MESH = pl.DeviceIdType.MESH


AHEAD_TIMES = ((0.25, 0.55), (0.75, 1.0))
BACK_TIMES = ((0.17, 0.4, 0.6), (0.5, 0.8, 1.0))


def schedule():
    events = []
    for what, pieces, times in (("ahead", FORWARD, AHEAD_TIMES), ("back", BACKWARD, BACK_TIMES)):
        for kv in (0, 1):
            for hop, time in enumerate(times[kv]):
                for i in range(len(pieces)):
                    events.append((time - 0.12 * (1 - (i + 1) / len(pieces)), what, kv, hop, i))
    return [event[1:] for event in sorted(events)]


def kernel(
    seq_size,
    total,
    len_ref,
    q_ref,
    k_ref,
    v_ref,
    o_ref,
    q_own,
    window,
    transit,
    scores,
    weights,
    peaks,
    inverse,
    bias,
    local_sem,
    z_send,
    y_send,
    ahead_sem,
    back_sem,
    y_sem,
):
    dp = lax.axis_index("dp")
    seq = lax.axis_index("seq")
    chunk = dp * seq_size + seq
    lane_y = seq % 4

    def at_chunk(offset):
        other = (chunk + offset + total) % total
        return (other // seq_size, other % seq_size)

    def at_y(turn):
        return (dp, seq - lane_y + (lane_y + turn) % 4)

    own = [
        pltpu.make_async_copy(q_ref, q_own, local_sem.at[0]),
        pltpu.make_async_copy(k_ref, window.at[0, 0], local_sem.at[1]),
        pltpu.make_async_copy(v_ref, window.at[1, 0], local_sem.at[2]),
    ]
    for copy in own:
        copy.start()

    barrier = pltpu.get_barrier_semaphore()
    for device in (at_chunk(-4), at_chunk(4), at_chunk(-12), at_y(1), at_y(2), at_y(3)):
        pl.semaphore_signal(barrier, inc=1, device_id=device, device_id_type=MESH)

    mine = (k_ref, v_ref)

    def passing_rows(piece):
        first, count = piece
        return pl.ds(first - BACK_FIRST, count)

    def send_ahead(kv, hop, i):
        rows = pl.ds(*FORWARD[i])
        pltpu.make_async_remote_copy(
            src_ref=mine[kv].at[rows] if hop == 0 else window.at[kv, 4, rows],
            dst_ref=window.at[kv, 4 + 4 * hop, rows],
            send_sem=z_send.at[kv, hop],
            recv_sem=ahead_sem.at[kv, hop, i],
            device_id=at_chunk(4),
            device_id_type=MESH,
        ).start()

    def send_back(kv, hop, i):
        rows = pl.ds(*BACKWARD[i])
        passed = transit.at[kv, passing_rows(BACKWARD[i])]
        pltpu.make_async_remote_copy(
            src_ref=(mine[kv].at[rows], passed, window.at[kv, 8, rows])[hop],
            dst_ref=(passed, window.at[kv, 8, rows], window.at[kv, 4, rows])[hop],
            send_sem=z_send.at[kv, hop],
            recv_sem=back_sem.at[kv, hop, i],
            device_id=at_chunk((-4, 12, -4)[hop]),
            device_id_type=MESH,
        ).start()

    def y_copy(kv, turn, message, src, rows):
        slot = turn + 4 * message
        return pltpu.make_async_remote_copy(
            src_ref=src,
            dst_ref=window.at[kv, slot, rows],
            send_sem=y_send.at[kv, turn - 1, message],
            recv_sem=y_sem.at[kv, slot],
            device_id=at_y(turn),
            device_id_type=MESH,
        )

    def share(kv, slot, rows):
        src = mine[kv].at[rows] if slot == 0 else window.at[kv, slot, rows]
        for turn in (1, 2, 3):
            ahead = lane_y + turn < 4
            if slot < 8:

                @pl.when(ahead)
                def _():
                    y_copy(kv, turn, slot // 4, src, rows).start()

            if slot > 0:

                @pl.when(jnp.logical_not(ahead))
                def _():
                    y_copy(kv, turn, slot // 4 - 1, src, rows).start()

    def arrive(what, kv, hop, i):
        rows = pl.ds(*(FORWARD if what == "ahead" else BACKWARD)[i])
        if what == "ahead":
            ref = window.at[kv, 4 + 4 * hop, rows]
            pltpu.make_async_copy(ref, ref, ahead_sem.at[kv, hop, i]).wait()
            if hop == 0:
                send_ahead(kv, 1, i)
                if kv == 0:
                    send_ahead(1, 0, i)
            share(kv, 4 + 4 * hop, rows)
        else:
            ref = (
                transit.at[kv, passing_rows(BACKWARD[i])],
                window.at[kv, 8, rows],
                window.at[kv, 4, rows],
            )[hop]
            pltpu.make_async_copy(ref, ref, back_sem.at[kv, hop, i]).wait()
            if hop < 2:
                send_back(kv, hop + 1, i)
            if hop > 0:
                share(kv, 12 - 4 * hop, rows)

    def await_slot(kv, slot):
        ref = window.at[kv, slot]
        pltpu.make_async_copy(ref, ref, y_sem.at[kv, slot]).wait()

    lengths = len_ref[...]
    count = lengths.shape[1]
    down = lax.broadcasted_iota(jnp.int32, (count, count), 0)
    across = lax.broadcasted_iota(jnp.int32, (count, count), 1)
    column = jnp.sum(jnp.where(down == across, lengths, 0), axis=1, keepdims=True)
    begins = jnp.sum(jnp.where(down < across, column, 0), axis=0, keepdims=True)
    base = chunk * ROWS
    positions = base + lax.broadcasted_iota(jnp.int32, (ROWS, 1), 0)
    starts = jnp.max(jnp.where(begins <= positions, begins, 0), axis=1, keepdims=True)
    key_lane = base + lax.broadcasted_iota(jnp.int32, (ROWS, ROWS), 1)
    for slot in range(SLOTS):
        keys_at = key_lane - slot * ROWS
        allowed = keys_at >= starts
        if slot == 0:
            allowed = allowed & (keys_at <= positions)
        bias[slot] = jnp.where(allowed, 0.0, MASKED)

    pl.semaphore_wait(barrier, 6)
    for i in range(len(FORWARD)):
        send_ahead(0, 0, i)
    for kv in (0, 1):
        for i in range(len(BACKWARD)):
            send_back(kv, 0, i)
    for kv in (0, 1):
        share(kv, 0, pl.ds(0, ROWS))

    for copy in own:
        copy.wait()

    def score(first, slots):
        @pl.loop(0, KVH)
        def _(head):
            column = pl.multiple_of(head * HD, HD)
            stacked = jnp.concatenate(
                [q_own[:, pl.ds(pl.multiple_of(head * GROUP * HD + j * HD, HD), HD)] for j in range(GROUP)],
                axis=0,
            )
            peak = None if first == 0 else peaks[head]
            keys = window[0, pl.ds(first, slots), :, pl.ds(column, HD)].reshape(slots * ROWS, HD)
            raw = lax.dot_general(
                stacked, keys, (((1,), (1,)), ((), ())), preferred_element_type=jnp.float32
            ).reshape(GROUP, ROWS, slots * ROWS)
            for i in range(slots):
                masked = raw[:, :, i * ROWS : (i + 1) * ROWS] + bias[first + i][None]
                scores[first + i, head] = masked
                peak = masked if peak is None else jnp.maximum(peak, masked)
            peaks[head] = peak

    def weigh(head):
        @pl.loop(0, GROUP)
        def _(j):
            peak = jnp.max(peaks[head, j], axis=1, keepdims=True)
            total_weight = jnp.zeros((ROWS, ROWS), jnp.float32)
            for slot in range(SLOTS):
                weight = jnp.exp2((scores[slot, head, j] - peak) * SCALE)
                total_weight = total_weight + weight
                weights[head, j, :, slot * ROWS : (slot + 1) * ROWS] = weight.astype(jnp.bfloat16)
            row_sum = jnp.sum(total_weight, axis=1, keepdims=True)
            inverse[head * GROUP + j] = jnp.broadcast_to(1.0 / row_sum, (ROWS, HD))

    score(0, 1)

    def mix(head, slots):
        values = jnp.concatenate([window[1, slot, :, pl.ds(pl.multiple_of(head * HD, HD), HD)] for slot in slots], axis=0)
        shares = jnp.concatenate([weights[head, :, :, slot * ROWS : (slot + 1) * ROWS] for slot in slots], axis=2)
        return jnp.dot(
            shares.reshape(GROUP * ROWS, len(slots) * ROWS), values, preferred_element_type=jnp.float32
        ).reshape(GROUP, ROWS, HD)

    events = schedule()
    keys_last = max(i for i, event in enumerate(events) if event[1] == 0)
    work = [functools.partial(score, first, 2) for first in (1, 3, 5, 7)]
    work += [functools.partial(weigh, head) for head in range(KVH)]
    last = [i for i in range(keys_last, len(events)) if events[i][2] < 2 - (events[i][0] == "ahead")]
    for i, event in enumerate(events):
        arrive(*event)
        if i == keys_last:
            for slot in (1, 2, 3, 5, 6, 7):
                await_slot(0, slot)
        if i in last:
            done = 8 * (last.index(i) + 1) // len(last) - 8 * last.index(i) // len(last)
            for _ in range(done):
                work.pop(0)()
    for step in work:
        step()

    along_y = (1, 2, 3, 5, 6, 7)

    @pl.loop(0, KVH)
    def _(head):
        peaks[head] = mix(head, (0, 4, 8))

    for slot in along_y:
        await_slot(1, slot)

    @pl.loop(0, KVH)
    def _(head):
        mixed = peaks[head] + mix(head, along_y)
        for j in range(GROUP):
            place = pl.multiple_of(head * GROUP * HD + j * HD, HD)
            o_ref[:, pl.ds(place, HD)] = (mixed[j] * inverse[head * GROUP + j]).astype(jnp.bfloat16)

    for kv in (0, 1):
        whole = window.at[kv, 0]
        for hop in (0, 1):
            pltpu.make_async_copy(whole, whole, z_send.at[kv, hop]).wait()
        pltpu.make_async_copy(transit.at[kv], transit.at[kv], z_send.at[kv, 2]).wait()
        for turn in (1, 2, 3):
            for message in (0, 1):
                pltpu.make_async_copy(whole, whole, y_send.at[kv, turn - 1, message]).wait()


def body(queries, key_proj, value_proj, seq_lengths):
    seq_size = lax.axis_size("seq")
    total = lax.axis_size("dp") * seq_size
    return pl.pallas_call(
        functools.partial(kernel, seq_size, total),
        out_shape=jax.ShapeDtypeStruct((ROWS, QH * HD), jnp.bfloat16),
        in_specs=[
            pl.BlockSpec(memory_space=pltpu.VMEM),
            pl.BlockSpec(memory_space=pl.ANY),
            pl.BlockSpec(memory_space=pl.ANY),
            pl.BlockSpec(memory_space=pl.ANY),
        ],
        out_specs=pl.BlockSpec(memory_space=pltpu.VMEM),
        scratch_shapes=[
            pltpu.VMEM((ROWS, QH * HD), jnp.bfloat16),
            pltpu.VMEM((2, SLOTS, ROWS, KVH * HD), jnp.bfloat16),
            pltpu.VMEM((2, ROWS - BACK_FIRST, KVH * HD), jnp.bfloat16),
            pltpu.VMEM((SLOTS, KVH, GROUP, ROWS, ROWS), jnp.float32),
            pltpu.VMEM((KVH, GROUP, ROWS, SLOTS * ROWS), jnp.bfloat16),
            pltpu.VMEM((KVH, GROUP, ROWS, ROWS), jnp.float32),
            pltpu.VMEM((QH, ROWS, HD), jnp.float32),
            pltpu.VMEM((SLOTS, ROWS, ROWS), jnp.float32),
            pltpu.SemaphoreType.DMA((3,)),
            pltpu.SemaphoreType.DMA((2, 3)),
            pltpu.SemaphoreType.DMA((2, 3, 2)),
            pltpu.SemaphoreType.DMA((2, 2, len(FORWARD))),
            pltpu.SemaphoreType.DMA((2, 3, len(BACKWARD))),
            pltpu.SemaphoreType.DMA((2, SLOTS)),
        ],
        compiler_params=pltpu.CompilerParams(
            collective_id=0, has_side_effects=True, vmem_limit_bytes=60 * 2**20
        ),
    )(seq_lengths.reshape(1, -1), queries, key_proj, value_proj)


def solution(mesh):
    return jax.shard_map(
        body,
        mesh=mesh,
        in_specs=(P(("dp", "seq"), None), P(("dp", "seq"), None), P(("dp", "seq"), None), P()),
        out_specs=P(("dp", "seq"), None),
        check_vma=False,
    )
```

```python
import functools

import jax
import jax.numpy as jnp
from jax import lax
from jax.experimental import pallas as pl
from jax.experimental.pallas import tpu as pltpu
from jax.sharding import PartitionSpec as P

HD = 128
QH = 32
KVH = 4
GROUP = QH // KVH
ROWS = 128
SLOTS = 9
FORWARD = ((0, 48), (48, 32))
BACKWARD = ((80, 32), (112, 16))
BACK_FIRST = BACKWARD[0][0]
SCALE = 0.08838834764831845 * 1.4426950408889634
MASKED = -1e30
MESH = pl.DeviceIdType.MESH


AHEAD_TIMES = ((0.25, 0.55), (0.75, 1.0))
BACK_TIMES = ((0.17, 0.4, 0.6), (0.5, 0.8, 1.0))


def schedule():
    events = []
    for what, pieces, times in (("ahead", FORWARD, AHEAD_TIMES), ("back", BACKWARD, BACK_TIMES)):
        for kv in (0, 1):
            for hop, time in enumerate(times[kv]):
                for i in range(len(pieces)):
                    events.append((time - 0.12 * (1 - (i + 1) / len(pieces)), what, kv, hop, i))
    return [event[1:] for event in sorted(events)]


def kernel(
    seq_size,
    total,
    len_ref,
    q_ref,
    k_ref,
    v_ref,
    o_ref,
    lengths_own,
    q_own,
    window,
    transit,
    scores,
    weights,
    peaks,
    inverse,
    bias,
    local_sem,
    z_send,
    y_send,
    ahead_sem,
    back_sem,
    y_sem,
):
    dp = lax.axis_index("dp")
    seq = lax.axis_index("seq")
    chunk = dp * seq_size + seq
    lane_y = seq % 4

    def at_chunk(offset):
        other = (chunk + offset + total) % total
        return (other // seq_size, other % seq_size)

    def at_y(turn):
        return (dp, seq - lane_y + (lane_y + turn) % 4)

    own = [
        pltpu.make_async_copy(len_ref, lengths_own, local_sem.at[3]),
        pltpu.make_async_copy(q_ref, q_own, local_sem.at[0]),
        pltpu.make_async_copy(k_ref, window.at[0, 0], local_sem.at[1]),
        pltpu.make_async_copy(v_ref, window.at[1, 0], local_sem.at[2]),
    ]
    for copy in own:
        copy.start()

    barrier = pltpu.get_barrier_semaphore()
    for device in (at_chunk(-4), at_chunk(4), at_chunk(-12), at_y(1), at_y(2), at_y(3)):
        pl.semaphore_signal(barrier, inc=1, device_id=device, device_id_type=MESH)

    mine = (k_ref, v_ref)

    def passing_rows(piece):
        first, count = piece
        return pl.ds(first - BACK_FIRST, count)

    def send_ahead(kv, hop, i):
        rows = pl.ds(*FORWARD[i])
        pltpu.make_async_remote_copy(
            src_ref=mine[kv].at[rows] if hop == 0 else window.at[kv, 4, rows],
            dst_ref=window.at[kv, 4 + 4 * hop, rows],
            send_sem=z_send.at[kv, hop],
            recv_sem=ahead_sem.at[kv, hop, i],
            device_id=at_chunk(4),
            device_id_type=MESH,
        ).start()

    def send_back(kv, hop, i):
        rows = pl.ds(*BACKWARD[i])
        passed = transit.at[kv, passing_rows(BACKWARD[i])]
        pltpu.make_async_remote_copy(
            src_ref=(mine[kv].at[rows], passed, window.at[kv, 8, rows])[hop],
            dst_ref=(passed, window.at[kv, 8, rows], window.at[kv, 4, rows])[hop],
            send_sem=z_send.at[kv, hop],
            recv_sem=back_sem.at[kv, hop, i],
            device_id=at_chunk((-4, 12, -4)[hop]),
            device_id_type=MESH,
        ).start()

    def y_copy(kv, turn, message, src, rows):
        slot = turn + 4 * message
        return pltpu.make_async_remote_copy(
            src_ref=src,
            dst_ref=window.at[kv, slot, rows],
            send_sem=y_send.at[kv, turn - 1, message],
            recv_sem=y_sem.at[kv, slot],
            device_id=at_y(turn),
            device_id_type=MESH,
        )

    def share(kv, slot, rows):
        src = mine[kv].at[rows] if slot == 0 else window.at[kv, slot, rows]
        for turn in (1, 2, 3):
            ahead = lane_y + turn < 4
            if slot < 8:

                @pl.when(ahead)
                def _():
                    y_copy(kv, turn, slot // 4, src, rows).start()

            if slot > 0:

                @pl.when(jnp.logical_not(ahead))
                def _():
                    y_copy(kv, turn, slot // 4 - 1, src, rows).start()

    def arrive(what, kv, hop, i):
        rows = pl.ds(*(FORWARD if what == "ahead" else BACKWARD)[i])
        if what == "ahead":
            ref = window.at[kv, 4 + 4 * hop, rows]
            pltpu.make_async_copy(ref, ref, ahead_sem.at[kv, hop, i]).wait()
            if hop == 0:
                send_ahead(kv, 1, i)
                if kv == 0:
                    send_ahead(1, 0, i)
            share(kv, 4 + 4 * hop, rows)
        else:
            ref = (
                transit.at[kv, passing_rows(BACKWARD[i])],
                window.at[kv, 8, rows],
                window.at[kv, 4, rows],
            )[hop]
            pltpu.make_async_copy(ref, ref, back_sem.at[kv, hop, i]).wait()
            if hop < 2:
                send_back(kv, hop + 1, i)
            if hop > 0:
                share(kv, 12 - 4 * hop, rows)

    def await_slot(kv, slot):
        ref = window.at[kv, slot]
        pltpu.make_async_copy(ref, ref, y_sem.at[kv, slot]).wait()

    own[0].wait()
    lengths = lengths_own[...]
    count = lengths.shape[1]
    down = lax.broadcasted_iota(jnp.int32, (count, count), 0)
    across = lax.broadcasted_iota(jnp.int32, (count, count), 1)
    column = jnp.sum(jnp.where(down == across, lengths, 0), axis=1, keepdims=True)
    begins = jnp.sum(jnp.where(down < across, column, 0), axis=0, keepdims=True)
    base = chunk * ROWS
    positions = base + lax.broadcasted_iota(jnp.int32, (ROWS, 1), 0)
    starts = jnp.max(jnp.where(begins <= positions, begins, 0), axis=1, keepdims=True)
    key_lane = base + lax.broadcasted_iota(jnp.int32, (ROWS, ROWS), 1)
    for slot in range(SLOTS):
        keys_at = key_lane - slot * ROWS
        allowed = keys_at >= starts
        if slot == 0:
            allowed = allowed & (keys_at <= positions)
        bias[slot] = jnp.where(allowed, 0.0, MASKED)

    pl.semaphore_wait(barrier, 6)
    for i in range(len(FORWARD)):
        send_ahead(0, 0, i)
    for kv in (0, 1):
        for i in range(len(BACKWARD)):
            send_back(kv, 0, i)
    for kv in (0, 1):
        share(kv, 0, pl.ds(0, ROWS))

    for copy in own[1:]:
        copy.wait()

    def score(first, slots):
        @pl.loop(0, KVH)
        def _(head):
            column = pl.multiple_of(head * HD, HD)
            stacked = jnp.concatenate(
                [q_own[:, pl.ds(pl.multiple_of(head * GROUP * HD + j * HD, HD), HD)] for j in range(GROUP)],
                axis=0,
            )
            peak = None if first == 0 else peaks[head]
            keys = window[0, pl.ds(first, slots), :, pl.ds(column, HD)].reshape(slots * ROWS, HD)
            raw = lax.dot_general(
                stacked, keys, (((1,), (1,)), ((), ())), preferred_element_type=jnp.float32
            ).reshape(GROUP, ROWS, slots * ROWS)
            for i in range(slots):
                masked = raw[:, :, i * ROWS : (i + 1) * ROWS] * SCALE + bias[first + i][None]
                scores[first + i, head] = masked
                peak = masked if peak is None else jnp.maximum(peak, masked)
            peaks[head] = peak

    def weigh(head):
        @pl.loop(0, GROUP)
        def _(j):
            peak = jnp.max(peaks[head, j], axis=1, keepdims=True)
            total_weight = jnp.zeros((ROWS, ROWS), jnp.float32)
            for slot in range(SLOTS):
                weight = jnp.exp2(scores[slot, head, j] - peak)
                total_weight = total_weight + weight
                weights[head, j, :, slot * ROWS : (slot + 1) * ROWS] = weight.astype(jnp.bfloat16)
            row_sum = jnp.sum(total_weight, axis=1, keepdims=True)
            inverse[head * GROUP + j] = jnp.broadcast_to(1.0 / row_sum, (ROWS, HD))

    score(0, 1)

    def mix(head, slots):
        values = jnp.concatenate([window[1, slot, :, pl.ds(pl.multiple_of(head * HD, HD), HD)] for slot in slots], axis=0)
        shares = jnp.concatenate([weights[head, :, :, slot * ROWS : (slot + 1) * ROWS] for slot in slots], axis=2)
        return jnp.dot(
            shares.reshape(GROUP * ROWS, len(slots) * ROWS), values, preferred_element_type=jnp.float32
        ).reshape(GROUP, ROWS, HD)

    events = schedule()
    keys_last = max(i for i, event in enumerate(events) if event[1] == 0)
    work = [functools.partial(score, first, 2) for first in (1, 3, 5, 7)]
    work += [functools.partial(weigh, head) for head in range(KVH)]
    last = [i for i in range(keys_last, len(events)) if events[i][2] < 2 - (events[i][0] == "ahead")]
    for i, event in enumerate(events):
        arrive(*event)
        if i == keys_last:
            for slot in (1, 2, 3, 5, 6, 7):
                await_slot(0, slot)
        if i in last:
            done = 8 * (last.index(i) + 1) // len(last) - 8 * last.index(i) // len(last)
            for _ in range(done):
                work.pop(0)()
    for step in work:
        step()

    along_y = (1, 2, 3, 5, 6, 7)

    @pl.loop(0, KVH)
    def _(head):
        peaks[head] = mix(head, (0, 4, 8))

    for slot in along_y:
        await_slot(1, slot)

    @pl.loop(0, KVH)
    def _(head):
        mixed = peaks[head] + mix(head, along_y)
        for j in range(GROUP):
            place = pl.multiple_of(head * GROUP * HD + j * HD, HD)
            o_ref[:, pl.ds(place, HD)] = (mixed[j] * inverse[head * GROUP + j]).astype(jnp.bfloat16)

    for kv in (0, 1):
        whole = window.at[kv, 0]
        for hop in (0, 1):
            pltpu.make_async_copy(whole, whole, z_send.at[kv, hop]).wait()
        pltpu.make_async_copy(transit.at[kv], transit.at[kv], z_send.at[kv, 2]).wait()
        for turn in (1, 2, 3):
            for message in (0, 1):
                pltpu.make_async_copy(whole, whole, y_send.at[kv, turn - 1, message]).wait()


def body(queries, key_proj, value_proj, seq_lengths):
    seq_size = lax.axis_size("seq")
    total = lax.axis_size("dp") * seq_size
    return pl.pallas_call(
        functools.partial(kernel, seq_size, total),
        out_shape=jax.ShapeDtypeStruct((ROWS, QH * HD), jnp.bfloat16),
        in_specs=[
            pl.BlockSpec(memory_space=pltpu.HBM),
            pl.BlockSpec(memory_space=pltpu.HBM),
            pl.BlockSpec(memory_space=pltpu.HBM),
            pl.BlockSpec(memory_space=pltpu.HBM),
        ],
        out_specs=pl.BlockSpec(memory_space=pltpu.VMEM),
        scratch_shapes=[
            pltpu.VMEM((1, seq_lengths.shape[0]), jnp.int32),
            pltpu.VMEM((ROWS, QH * HD), jnp.bfloat16),
            pltpu.VMEM((2, SLOTS, ROWS, KVH * HD), jnp.bfloat16),
            pltpu.VMEM((2, ROWS - BACK_FIRST, KVH * HD), jnp.bfloat16),
            pltpu.VMEM((SLOTS, KVH, GROUP, ROWS, ROWS), jnp.float32),
            pltpu.VMEM((KVH, GROUP, ROWS, SLOTS * ROWS), jnp.bfloat16),
            pltpu.VMEM((KVH, GROUP, ROWS, ROWS), jnp.float32),
            pltpu.VMEM((QH, ROWS, HD), jnp.float32),
            pltpu.VMEM((SLOTS, ROWS, ROWS), jnp.float32),
            pltpu.SemaphoreType.DMA((4,)),
            pltpu.SemaphoreType.DMA((2, 3)),
            pltpu.SemaphoreType.DMA((2, 3, 2)),
            pltpu.SemaphoreType.DMA((2, 2, len(FORWARD))),
            pltpu.SemaphoreType.DMA((2, 3, len(BACKWARD))),
            pltpu.SemaphoreType.DMA((2, SLOTS)),
        ],
        compiler_params=pltpu.CompilerParams(
            collective_id=0, has_side_effects=True, vmem_limit_bytes=60 * 2**20
        ),
    )(seq_lengths.reshape(1, -1), queries, key_proj, value_proj)


def solution(mesh):
    return jax.shard_map(
        body,
        mesh=mesh,
        in_specs=(P(("dp", "seq"), None), P(("dp", "seq"), None), P(("dp", "seq"), None), P()),
        out_specs=P(("dp", "seq"), None),
        check_vma=False,
    )
```
